32 devices in a mesh: row: 4 (over x, core), col: 8 (over z, y).
Axes of the slice: x: 2, y: 2, z: 4, core: 2. Of those that a mesh axis runs over, the one named last changes fastest.
Arguments:
- tokens: bfloat16 [768, 6144], P('row', 'col'), may hold values from -6 to 6
- out_grad: bfloat16 [768, 6144], P('row', 'col'), may hold values from -6 to 6
- w_up: bfloat16 [6144, 24576], P('col', 'row'), may hold values from -0.078125 to 0.078125
- w_down: bfloat16 [24576, 6144], P('row', 'col'), may hold values from -0.078125 to 0.078125
- mask_up: int32 [96, 384], P('col', 'row'), may hold values from 0 to 1, as said below
- mask_down: int32 [384, 96], P('row', 'col'), may hold values from 0 to 1, as said below
- acc_up: float32 [6144, 24576], P('col', 'row'), may hold values from -96 to 96
- acc_down: float32 [24576, 6144], P('row', 'col'), may hold values from -96 to 96
Outputs:
- in_grad: bfloat16 [768, 6144], P('row', 'col')
- new_acc_up: float32 [6144, 24576], P('col', 'row')
- new_acc_down: float32 [24576, 6144], P('row', 'col')
The draws below stay inside these ranges and needn't reach their ends.
Inputs may be any that keep to these rules, and one draw needn't show every extreme that they name: `mask_up`: each entry is 0 (pruned block) or 1 (kept block); the share of kept blocks varies between block rows and block columns. `mask_down`: each entry is 0 (pruned block) or 1 (kept block); the share of kept blocks varies between block rows and block columns.
All inputs are finite; a program needn't handle non-finite values.
Results may differ from the reference program's by a relative error of at most 0.028.
Values may be sent and summed in bfloat16 or wider, within the bound.
A program may use at most 256 MiB of HBM per device.

```python
import math
import jax
import jax.numpy as jnp
from jax import lax

D = 6144
FF = 24576
BLK = 64
TOKENS = 768
FEAT_BLOCK = 768
N_COL = 8


def block_pattern(seed_key, rows, cols):
    keys = jax.random.split(seed_key, 3)
    row_level = jax.random.randint(keys[0], (rows, 1), 10, 50)
    col_level = jax.random.randint(keys[1], (1, cols), 10, 50)
    values = jax.random.randint(keys[2], (rows, cols), 0, 100)
    return jnp.where(values < row_level + col_level, 1, 0).astype(jnp.int32)


def draw_mask_up(key, part):
    return block_pattern(jax.random.fold_in(key, 11), D // BLK, FF // BLK)


def draw_mask_down(key, part):
    return block_pattern(jax.random.fold_in(key, 23), FF // BLK, D // BLK)


def block_levels(own_key, extent, cuts, low, high):
    factor_of, own = 1.0, jax.random.fold_in(own_key, 6)
    for position, blocks in cuts:
        steps = jnp.exp(jax.random.uniform(jax.random.fold_in(own, position), (blocks,), jnp.float32, low / len(cuts), high / len(cuts)))
        factor_of = factor_of * jnp.repeat(steps, extent[position] // blocks).reshape([-1 if axis == position else 1 for axis in range(len(extent))])
    return factor_of


def scatter_about(own_key, dims, scale, most, cuts=(), dtype=jnp.bfloat16):
    entries = jax.random.normal(own_key, dims, jnp.float32) * scale
    if len(cuts) > 0:
        entries = block_levels(own_key, dims, cuts, -0.22, 0.18) * entries
    return jnp.clip(entries, min=-most, max=most).astype(dtype)


def setup_inputs(seed: int = 0) -> dict:
    arg_keys = jax.random.split(jax.random.key(seed), 9)
    return {
        "tokens": scatter_about(arg_keys[0], (TOKENS, D), 1.0, 6.0, ((0, 4), (1, 8))),
        "out_grad": scatter_about(arg_keys[1], (TOKENS, D), 1.0, 6.0, ((0, 4), (1, 8))),
        "w_up": scatter_about(arg_keys[2], (D, FF), D ** -0.5, 0.078125, ((0, 8), (1, 4))),
        "w_down": scatter_about(arg_keys[3], (FF, D), D ** -0.5, 0.078125, ((0, 4), (1, 8))),
        "mask_up": draw_mask_up(jax.random.fold_in(arg_keys[8], 71), 0),
        "mask_down": draw_mask_down(jax.random.fold_in(arg_keys[8], 71), 0),
        "acc_up": scatter_about(arg_keys[6], (D, FF), 16.0, 96.0, ((0, 8), (1, 4)), jnp.float32),
        "acc_down": scatter_about(arg_keys[7], (FF, D), 16.0, 96.0, ((0, 4), (1, 8)), jnp.float32),
    }


def spread_mask(mask_grid):
    rows, cols = mask_grid.shape
    full = jnp.broadcast_to(mask_grid[:, None, :, None], (rows, BLK, cols, BLK))
    return full.reshape(rows * BLK, cols * BLK).astype(jnp.bfloat16)

def gelu_parts(value):
    cdf = 0.5 * (1.0 + jax.scipy.special.erf(value / math.sqrt(2.0)))
    pdf = jnp.exp(-0.5 * value * value) / math.sqrt(2.0 * math.pi)
    return (value * cdf, cdf + value * pdf)

def reference(tokens, out_grad, w_up, w_down, mask_up, mask_down, acc_up, acc_down):
    up_eff = w_up * spread_mask(mask_up)
    down_eff = w_down * spread_mask(mask_down)
    pre = jnp.zeros((TOKENS, FF), jnp.float32)
    back = jnp.zeros((TOKENS, FF), jnp.float32)
    for index in range(N_COL):
        lower = index * FEAT_BLOCK
        upper = lower + FEAT_BLOCK
        part_pre = jnp.dot(tokens[:, lower:upper], up_eff[lower:upper, :], preferred_element_type=jnp.float32)
        part_back = jnp.dot(out_grad[:, lower:upper], down_eff[:, lower:upper].T, preferred_element_type=jnp.float32)
        part_pre = lax.optimization_barrier(part_pre.astype(jnp.bfloat16))
        part_back = lax.optimization_barrier(part_back.astype(jnp.bfloat16))
        pre = pre + part_pre.astype(jnp.float32)
        back = back + part_back.astype(jnp.float32)
    act_value, act_slope = gelu_parts(pre)
    hidden = act_value.astype(jnp.bfloat16)
    pre_grad = (back * act_slope).astype(jnp.bfloat16)
    grad_up = jnp.dot(tokens.T, pre_grad, preferred_element_type=jnp.float32)
    new_acc_up = acc_up + spread_mask(mask_up).astype(jnp.float32) * grad_up
    grad_down = jnp.dot(hidden.T, out_grad, preferred_element_type=jnp.float32)
    new_acc_down = acc_down + spread_mask(mask_down).astype(jnp.float32) * grad_down
    in_grad = jnp.dot(pre_grad, up_eff.T, preferred_element_type=jnp.float32).astype(jnp.bfloat16)
    return (in_grad, new_acc_up, new_acc_down)
```

```python
import math

import jax
import jax.numpy as jnp
from jax import lax
from jax.sharding import PartitionSpec as P


def gelu_parts(value):
    cdf = 0.5 * (1.0 + jax.scipy.special.erf(value / math.sqrt(2.0)))
    pdf = jnp.exp(-0.5 * value * value) / math.sqrt(2.0 * math.pi)
    return (value * cdf, cdf + value * pdf)


def dot_f32(left, right, left_dim, right_dim):
    return lax.dot_general(
        left, right, (((left_dim,), (right_dim,)), ((), ())), preferred_element_type=jnp.float32
    )


def spread_block(mask_block, block_size):
    rows, cols = mask_block.shape

    def repeat(count):
        at = lax.broadcasted_iota(jnp.int32, (count * block_size, count), 0) // block_size
        return (at == lax.broadcasted_iota(jnp.int32, (count * block_size, count), 1)).astype(jnp.bfloat16)

    tall = dot_f32(repeat(rows), mask_block.astype(jnp.bfloat16), 1, 0).astype(jnp.bfloat16)
    return dot_f32(tall, repeat(cols), 1, 1).astype(jnp.bfloat16)


def ring_order(size):
    return list(range(0, size, 2)) + list(range(size - 1, 0, -2))


def make_local(n_col):
    order = ring_order(n_col)
    ahead = [(order[i], order[(i + 1) % n_col]) for i in range(n_col)]
    behind = [(order[(i + 1) % n_col], order[i]) for i in range(n_col)]
    place = [order.index(i) for i in range(n_col)]

    def local(tokens, out_grad, w_up, w_down, mask_up, mask_down, acc_up, acc_down):
        block = w_up.shape[0] // mask_up.shape[0]
        hidden_cols = w_up.shape[1]
        halves = 2 if hidden_cols // n_col % (2 * block) == 0 else 1
        width = hidden_cols // n_col // halves
        blocks = width // block
        me = jnp.array(place, jnp.int32)[lax.axis_index("col")]
        x_all = lax.all_gather(tokens, "row", axis=0, tiled=True)
        g_all = lax.all_gather(out_grad, "row", axis=0, tiled=True)

        def fwd(value):
            return lax.ppermute(value, "col", ahead)

        def bwd(value):
            return lax.ppermute(value, "col", behind)

        def up_at(j, h):
            return lax.rem(me - j + n_col, n_col) * halves + h

        def down_at(j, h):
            return lax.rem(me + j, n_col) * halves + h

        up_mask, down_mask, up_eff, down_eff = {}, {}, {}, {}

        def up_piece(j, h):
            at = up_at(j, h)
            m = spread_block(lax.dynamic_slice_in_dim(mask_up, at * blocks, blocks, 1), block)
            up_mask[j, h] = m
            up_eff[j, h] = lax.dynamic_slice_in_dim(w_up, at * width, width, 1) * m
            return dot_f32(x_all, up_eff[j, h], 1, 0)

        def down_piece(j, h):
            at = down_at(j, h)
            m = spread_block(lax.dynamic_slice_in_dim(mask_down, at * blocks, blocks, 0), block)
            down_mask[j, h] = m
            down_eff[j, h] = lax.dynamic_slice_in_dim(w_down, at * width, width, 0) * m
            return dot_f32(g_all, down_eff[j, h], 1, 1)

        pre, back = {}, {}
        for j in list(range(1, n_col)) + [0]:
            for h in range(halves):
                part = up_piece(j, h)
                part = part if j == 1 else part + pre[h].astype(jnp.float32)
                pre[h] = part if j == 0 else fwd(part.astype(jnp.bfloat16))
                part = down_piece(j, h)
                part = part if j == 1 else part + back[h].astype(jnp.float32)
                back[h] = part if j == 0 else bwd(part.astype(jnp.bfloat16))

        hidden, pre_grad = {}, {}
        for h in range(halves):
            value, slope = gelu_parts(pre[h])
            hidden[h] = value.astype(jnp.bfloat16)
            pre_grad[h] = (back[h] * slope).astype(jnp.bfloat16)

        new_up = jnp.zeros_like(acc_up)
        new_down = jnp.zeros_like(acc_down)
        grad_in = None
        for j in range(n_col):
            for h in range(halves):
                next_grad = fwd(pre_grad[h]) if j < n_col - 1 else None
                next_hidden = bwd(hidden[h]) if j < n_col - 1 else None
                part = dot_f32(pre_grad[h], up_eff[j, h], 1, 1)
                grad_in = part if grad_in is None else grad_in + part
                at = up_at(j, h) * width
                piece = lax.dynamic_slice_in_dim(acc_up, at, width, 1) + up_mask[j, h].astype(
                    jnp.float32
                ) * dot_f32(x_all, pre_grad[h], 0, 0)
                new_up = lax.dynamic_update_slice_in_dim(new_up, piece, at, 1)
                at = down_at(j, h) * width
                piece = lax.dynamic_slice_in_dim(acc_down, at, width, 0) + down_mask[j, h].astype(
                    jnp.float32
                ) * dot_f32(hidden[h], g_all, 0, 0)
                new_down = lax.dynamic_update_slice_in_dim(new_down, piece, at, 0)
                pre_grad[h], hidden[h] = next_grad, next_hidden
        in_grad = lax.psum_scatter(
            grad_in.astype(jnp.bfloat16), "row", scatter_dimension=0, tiled=True
        )
        return (in_grad, new_up, new_down)

    return local


def solution(mesh):
    feats, hids = P("row", "col"), P("col", "row")
    return jax.shard_map(
        make_local(mesh.shape["col"]),
        mesh=mesh,
        in_specs=(feats, feats, hids, feats, hids, feats, hids, feats),
        out_specs=(feats, hids, feats),
        check_vma=False,
    )
```

```python
import functools
import math

import jax
import jax.numpy as jnp
from jax import lax
from jax.experimental import pallas as pl
from jax.experimental.pallas import tpu as pltpu
from jax.sharding import PartitionSpec as P


def gelu_parts(value):
    cdf = 0.5 * (1.0 + jax.scipy.special.erf(value / math.sqrt(2.0)))
    pdf = jnp.exp(-0.5 * value * value) / math.sqrt(2.0 * math.pi)
    return (value * cdf, cdf + value * pdf)


def dot_f32(left, right, left_dim, right_dim):
    return lax.dot_general(
        left, right, (((left_dim,), (right_dim,)), ((), ())), preferred_element_type=jnp.float32
    )


def mask_kernel(block, up_tall, down_wide, w_up, w_down, up_eff, down_eff, up_mask, down_mask, new_up, new_down):
    step = pl.program_id(0)
    count, width = up_tall.shape[1], w_up.shape[1]
    along = (lax.broadcasted_iota(jnp.int32, (count, width), 1) + step * width) // block
    pick = (along == lax.broadcasted_iota(jnp.int32, (count, width), 0)).astype(jnp.bfloat16)
    mask = dot_f32(up_tall[...], pick, 1, 0).astype(jnp.bfloat16)
    up_mask[...] = mask
    up_eff[...] = w_up[...] * mask
    mask = dot_f32(pick, down_wide[...], 0, 0).astype(jnp.bfloat16)
    down_mask[...] = mask
    down_eff[...] = w_down[...] * mask


def masked_weights(w_up, w_down, mask_up, mask_down):
    feats, hids = w_up.shape
    block = feats // mask_up.shape[0]
    tall = jnp.repeat(mask_up.astype(jnp.bfloat16), block, axis=0)
    wide = jnp.repeat(mask_down.astype(jnp.bfloat16), block, axis=1)
    width = hids // 8
    up_spec = pl.BlockSpec((feats, width), lambda i: (0, i))
    down_spec = pl.BlockSpec((width, feats), lambda i: (i, 0))
    up, down = jax.ShapeDtypeStruct(w_up.shape, jnp.bfloat16), jax.ShapeDtypeStruct(w_down.shape, jnp.bfloat16)
    return pl.pallas_call(
        functools.partial(mask_kernel, block),
        grid=(8,),
        in_specs=[
            pl.BlockSpec(tall.shape, lambda i: (0, 0)),
            pl.BlockSpec(wide.shape, lambda i: (0, 0)),
            up_spec,
            down_spec,
        ],
        out_specs=[up_spec, down_spec, up_spec, down_spec] + [pl.BlockSpec(memory_space=pl.ANY)] * 2,
        out_shape=[
            up,
            down,
            up,
            down,
            jax.ShapeDtypeStruct(w_up.shape, jnp.float32),
            jax.ShapeDtypeStruct(w_down.shape, jnp.float32),
        ],
        compiler_params=pltpu.CompilerParams(vmem_limit_bytes=40 * 2**20),
        cost_estimate=pl.CostEstimate(flops=4 * feats * hids * 128, bytes_accessed=12 * feats * hids, transcendentals=0),
    )(tall, wide, w_up, w_down)


def swap(value, bit, size):
    return lax.ppermute(value, "row", [(i, i ^ bit) for i in range(size)])


def gather_rows(value, size):
    if size != 4:
        return lax.all_gather(value, "row", axis=0, tiled=True)
    far = swap(value, 2, size)
    return jnp.concatenate([value, swap(value, 1, size), far, swap(far, 1, size)], axis=0)


def scatter_rows(total, size):
    if size != 4:
        return lax.psum_scatter(total.astype(jnp.bfloat16), "row", scatter_dimension=0, tiled=True)
    own, core, chip, both = jnp.split(total, 4, axis=0)
    chip = chip + swap(both.astype(jnp.bfloat16), 1, size).astype(jnp.float32)
    own = own + swap(core.astype(jnp.bfloat16), 1, size).astype(jnp.float32)
    return (own + swap(chip.astype(jnp.bfloat16), 2, size).astype(jnp.float32)).astype(jnp.bfloat16)


def ring_order(size):
    return list(range(0, size, 2)) + list(range(size - 1, 0, -2))


def make_local(n_row, n_col):
    order = ring_order(n_col)
    ahead = [(order[i], order[(i + 1) % n_col]) for i in range(n_col)]
    behind = [(order[(i + 1) % n_col], order[i]) for i in range(n_col)]
    place = [order.index(i) for i in range(n_col)]

    def local(tokens, out_grad, w_up, w_down, mask_up, mask_down, acc_up, acc_down):
        block = w_up.shape[0] // mask_up.shape[0]
        hidden_cols = w_up.shape[1]
        halves = 2 if hidden_cols // n_col % (2 * block) == 0 else 1
        width = hidden_cols // n_col // halves
        me = jnp.array(place, jnp.int32)[lax.axis_index("col")]
        x_all = gather_rows(tokens, n_row)
        g_all = gather_rows(out_grad, n_row)
        up_eff, down_eff, up_mask, down_mask, new_up, new_down = masked_weights(
            w_up, w_down, mask_up, mask_down
        )

        def fwd(value):
            return lax.ppermute(value, "col", ahead)

        def bwd(value):
            return lax.ppermute(value, "col", behind)

        def up_at(j, h):
            return lax.rem(me - j + n_col, n_col) * halves + h

        def down_at(j, h):
            return lax.rem(me + j, n_col) * halves + h

        def cols(array, j, h):
            return lax.dynamic_slice_in_dim(array, up_at(j, h) * width, width, 1)

        def rows(array, j, h):
            return lax.dynamic_slice_in_dim(array, down_at(j, h) * width, width, 0)

        pre, back = {}, {}
        for j in list(range(1, n_col)) + [0]:
            for h in range(halves):
                part = dot_f32(x_all, cols(up_eff, j, h), 1, 0)
                part = part if j == 1 else part + pre[h].astype(jnp.float32)
                pre[h] = part if j == 0 else fwd(part.astype(jnp.bfloat16))
                part = dot_f32(g_all, rows(down_eff, j, h), 1, 1)
                part = part if j == 1 else part + back[h].astype(jnp.float32)
                back[h] = part if j == 0 else bwd(part.astype(jnp.bfloat16))

        hidden, pre_grad = {}, {}
        for h in range(halves):
            value, slope = gelu_parts(pre[h])
            hidden[h] = value.astype(jnp.bfloat16)
            pre_grad[h] = (back[h] * slope).astype(jnp.bfloat16)

        grad_in = None
        for j in range(n_col):
            for h in range(halves):
                next_grad = fwd(pre_grad[h]) if j < n_col - 1 else None
                next_hidden = bwd(hidden[h]) if j < n_col - 1 else None
                part = dot_f32(pre_grad[h], cols(up_eff, j, h), 1, 1)
                grad_in = part if grad_in is None else lax.optimization_barrier(grad_in + part)
                piece = cols(acc_up, j, h) + cols(up_mask, j, h).astype(jnp.float32) * dot_f32(
                    x_all, pre_grad[h], 0, 0
                )
                new_up = lax.dynamic_update_slice_in_dim(new_up, piece, up_at(j, h) * width, 1)
                piece = rows(acc_down, j, h) + rows(down_mask, j, h).astype(jnp.float32) * dot_f32(
                    hidden[h], g_all, 0, 0
                )
                new_down = lax.dynamic_update_slice_in_dim(new_down, piece, down_at(j, h) * width, 0)
                pre_grad[h], hidden[h] = next_grad, next_hidden
        in_grad = scatter_rows(grad_in, n_row)
        return (in_grad, new_up, new_down)

    return local


def solution(mesh):
    feats, hids = P("row", "col"), P("col", "row")
    return jax.shard_map(
        make_local(mesh.shape["row"], mesh.shape["col"]),
        mesh=mesh,
        in_specs=(feats, feats, hids, feats, hids, feats, hids, feats),
        out_specs=(feats, hids, feats),
        check_vma=False,
    )
```

```python
import functools
import math

import jax
import jax.numpy as jnp
from jax import lax
from jax.experimental import pallas as pl
from jax.experimental.pallas import tpu as pltpu
from jax.sharding import PartitionSpec as P


def gelu_parts(value):
    cdf = 0.5 * (1.0 + jax.scipy.special.erf(value / math.sqrt(2.0)))
    pdf = jnp.exp(-0.5 * value * value) / math.sqrt(2.0 * math.pi)
    return (value * cdf, cdf + value * pdf)


def dot_f32(left, right, left_dim, right_dim):
    return lax.dot_general(
        left, right, (((left_dim,), (right_dim,)), ((), ())), preferred_element_type=jnp.float32
    )


def mask_kernel(block, up_tall, down_wide, w_up, w_down, up_eff, down_eff, up_mask, down_mask, new_up, new_down):
    step = pl.program_id(0)
    count, width = up_tall.shape[1], w_up.shape[1]
    along = (lax.broadcasted_iota(jnp.int32, (count, width), 1) + step * width) // block
    pick = (along == lax.broadcasted_iota(jnp.int32, (count, width), 0)).astype(jnp.bfloat16)
    mask = dot_f32(up_tall[...], pick, 1, 0).astype(jnp.bfloat16)
    up_mask[...] = mask
    up_eff[...] = w_up[...] * mask
    mask = dot_f32(pick, down_wide[...], 0, 0).astype(jnp.bfloat16)
    down_mask[...] = mask
    down_eff[...] = w_down[...] * mask


def masked_weights(w_up, w_down, mask_up, mask_down):
    feats, hids = w_up.shape
    block = feats // mask_up.shape[0]
    tall = jnp.repeat(mask_up.astype(jnp.bfloat16), block, axis=0)
    wide = jnp.repeat(mask_down.astype(jnp.bfloat16), block, axis=1)
    width = hids // 8
    up_spec = pl.BlockSpec((feats, width), lambda i: (0, i))
    down_spec = pl.BlockSpec((width, feats), lambda i: (i, 0))
    up, down = jax.ShapeDtypeStruct(w_up.shape, jnp.bfloat16), jax.ShapeDtypeStruct(w_down.shape, jnp.bfloat16)
    return pl.pallas_call(
        functools.partial(mask_kernel, block),
        grid=(8,),
        in_specs=[
            pl.BlockSpec(tall.shape, lambda i: (0, 0)),
            pl.BlockSpec(wide.shape, lambda i: (0, 0)),
            up_spec,
            down_spec,
        ],
        out_specs=[up_spec, down_spec, up_spec, down_spec] + [pl.BlockSpec(memory_space=pl.ANY)] * 2,
        out_shape=[
            up,
            down,
            up,
            down,
            jax.ShapeDtypeStruct(w_up.shape, jnp.float32),
            jax.ShapeDtypeStruct(w_down.shape, jnp.float32),
        ],
        compiler_params=pltpu.CompilerParams(vmem_limit_bytes=40 * 2**20),
        cost_estimate=pl.CostEstimate(flops=4 * feats * hids * 128, bytes_accessed=12 * feats * hids, transcendentals=0),
    )(tall, wide, w_up, w_down)


def up_kernel(at, x_all, grads, eff, mask, acc, total, _, new_total, new_acc, zero):
    zero[...] = jnp.zeros(zero.shape, zero.dtype)
    new_total[...] = total[...] + dot_f32(grads[...], eff[...], 1, 1)
    new_acc[...] = acc[...] + mask[...].astype(jnp.float32) * dot_f32(x_all[...], grads[...], 0, 0)


def down_kernel(at, hidden, g_all, mask, acc, _, new_acc, zero):
    zero[...] = jnp.zeros(zero.shape, zero.dtype)
    new_acc[...] = acc[...] + mask[...].astype(jnp.float32) * dot_f32(hidden[...], g_all[...], 0, 0)


ZERO = jax.ShapeDtypeStruct((16, 128), jnp.bfloat16)
SMALL = pl.CostEstimate(flops=1, bytes_accessed=1, transcendentals=0)


def up_step(at, x_all, grads, eff, mask, acc, total, new_acc):
    tokens, feats = x_all.shape
    width, tile = grads.shape[1], feats // 3
    piece = pl.BlockSpec((tile, width), lambda i, at: (i, at[0]))
    side = pl.BlockSpec((tokens, tile), lambda i, at: (0, i))
    whole = pl.BlockSpec(grads.shape, lambda i, at: (0, 0))
    return pl.pallas_call(
        up_kernel,
        grid_spec=pltpu.PrefetchScalarGridSpec(
            num_scalar_prefetch=1,
            grid=(3,),
            in_specs=[side, whole, piece, piece, piece, side, pl.BlockSpec(memory_space=pl.ANY)],
            out_specs=[side, piece, pl.BlockSpec(ZERO.shape, lambda i, at: (0, 0))],
        ),
        out_shape=[
            jax.ShapeDtypeStruct(total.shape, jnp.float32),
            jax.ShapeDtypeStruct(acc.shape, jnp.float32),
            ZERO,
        ],
        input_output_aliases={6: 0, 7: 1},
        compiler_params=pltpu.CompilerParams(vmem_limit_bytes=32 * 2**20),
        cost_estimate=SMALL,
    )(at.reshape(1), x_all, grads, eff, mask, acc, total, new_acc)


def down_step(at, hidden, g_all, mask, acc, new_acc):
    tokens, feats = g_all.shape
    width, tile = hidden.shape[1], feats // 3
    piece = pl.BlockSpec((width, tile), lambda i, at: (at[0], i))
    side = pl.BlockSpec((tokens, tile), lambda i, at: (0, i))
    whole = pl.BlockSpec(hidden.shape, lambda i, at: (0, 0))
    return pl.pallas_call(
        down_kernel,
        grid_spec=pltpu.PrefetchScalarGridSpec(
            num_scalar_prefetch=1,
            grid=(3,),
            in_specs=[whole, side, piece, piece, pl.BlockSpec(memory_space=pl.ANY)],
            out_specs=[piece, pl.BlockSpec(ZERO.shape, lambda i, at: (0, 0))],
        ),
        out_shape=[jax.ShapeDtypeStruct(acc.shape, jnp.float32), ZERO],
        input_output_aliases={5: 0},
        compiler_params=pltpu.CompilerParams(vmem_limit_bytes=32 * 2**20),
        cost_estimate=SMALL,
    )(at.reshape(1), hidden, g_all, mask, acc, new_acc)


def swap(value, bit, size):
    return lax.ppermute(value, "row", [(i, i ^ bit) for i in range(size)])


def gather_rows(value, size):
    if size != 4:
        return lax.all_gather(value, "row", axis=0, tiled=True)
    far = swap(value, 2, size)
    return jnp.concatenate([value, swap(value, 1, size), far, swap(far, 1, size)], axis=0)


def scatter_rows(total, size):
    if size != 4:
        return lax.psum_scatter(total.astype(jnp.bfloat16), "row", scatter_dimension=0, tiled=True)
    own, core, chip, both = jnp.split(total, 4, axis=0)
    chip = chip + swap(both.astype(jnp.bfloat16), 1, size).astype(jnp.float32)
    own = own + swap(core.astype(jnp.bfloat16), 1, size).astype(jnp.float32)
    return (own + swap(chip.astype(jnp.bfloat16), 2, size).astype(jnp.float32)).astype(jnp.bfloat16)


def ring_order(size):
    return list(range(0, size, 2)) + list(range(size - 1, 0, -2))


def make_local(n_row, n_col):
    order = ring_order(n_col)
    ahead = [(order[i], order[(i + 1) % n_col]) for i in range(n_col)]
    behind = [(order[(i + 1) % n_col], order[i]) for i in range(n_col)]
    place = [order.index(i) for i in range(n_col)]

    def local(tokens, out_grad, w_up, w_down, mask_up, mask_down, acc_up, acc_down):
        block = w_up.shape[0] // mask_up.shape[0]
        hidden_cols = w_up.shape[1]
        halves = 2 if hidden_cols // n_col % (2 * block) == 0 else 1
        width = hidden_cols // n_col // halves
        me = jnp.array(place, jnp.int32)[lax.axis_index("col")]
        x_all = gather_rows(tokens, n_row)
        g_all = gather_rows(out_grad, n_row)
        up_eff, down_eff, up_mask, down_mask, new_up, new_down = masked_weights(
            w_up, w_down, mask_up, mask_down
        )

        def fwd(value):
            return lax.ppermute(value, "col", ahead)

        def bwd(value):
            return lax.ppermute(value, "col", behind)

        def up_at(j, h):
            return lax.rem(me - j + n_col, n_col) * halves + h

        def down_at(j, h):
            return lax.rem(me + j, n_col) * halves + h

        def cols(array, j, h):
            return lax.dynamic_slice_in_dim(array, up_at(j, h) * width, width, 1)

        def rows(array, j, h):
            return lax.dynamic_slice_in_dim(array, down_at(j, h) * width, width, 0)

        pre, back = {}, {}
        for j in list(range(1, n_col)) + [0]:
            for h in range(halves):
                part = dot_f32(x_all, cols(up_eff, j, h), 1, 0)
                part = part if j == 1 else part + pre[h].astype(jnp.float32)
                pre[h] = part if j == 0 else fwd(part.astype(jnp.bfloat16))
                part = dot_f32(g_all, rows(down_eff, j, h), 1, 1)
                part = part if j == 1 else part + back[h].astype(jnp.float32)
                back[h] = part if j == 0 else bwd(part.astype(jnp.bfloat16))

        hidden, pre_grad = {}, {}
        for h in range(halves):
            value, slope = gelu_parts(pre[h])
            hidden[h] = value.astype(jnp.bfloat16)
            pre_grad[h] = (back[h] * slope).astype(jnp.bfloat16)

        after_up, after_down = [jnp.bfloat16(0)] * halves, [jnp.bfloat16(0)] * halves
        fused = width % 128 == 0 and w_up.shape[0] % 384 == 0
        grad_in = jnp.zeros((x_all.shape[0], w_up.shape[0]), jnp.float32) if fused else None
        for j in range(n_col):
            for h in range(halves):
                next_grad = fwd(pre_grad[h] + after_up[h]) if j < n_col - 1 else None
                next_hidden = bwd(hidden[h] + after_down[h]) if j < n_col - 1 else None
                if fused:
                    grad_in, new_up, zero_up = up_step(
                        up_at(j, h), x_all, pre_grad[h], up_eff, up_mask, acc_up, grad_in, new_up
                    )
                    new_down, zero_down = down_step(
                        down_at(j, h), hidden[h], g_all, down_mask, acc_down, new_down
                    )
                    after_up[h], after_down[h] = zero_up[0, 0], zero_down[0, 0]
                    pre_grad[h], hidden[h] = next_grad, next_hidden
                    continue
                part = dot_f32(pre_grad[h], cols(up_eff, j, h), 1, 1)
                grad_in = part if grad_in is None else lax.optimization_barrier(grad_in + part)
                piece = cols(acc_up, j, h) + cols(up_mask, j, h).astype(jnp.float32) * dot_f32(
                    x_all, pre_grad[h], 0, 0
                )
                new_up = lax.dynamic_update_slice_in_dim(new_up, piece, up_at(j, h) * width, 1)
                piece = rows(acc_down, j, h) + rows(down_mask, j, h).astype(jnp.float32) * dot_f32(
                    hidden[h], g_all, 0, 0
                )
                new_down = lax.dynamic_update_slice_in_dim(new_down, piece, down_at(j, h) * width, 0)
                pre_grad[h], hidden[h] = next_grad, next_hidden
        in_grad = scatter_rows(grad_in, n_row)
        return (in_grad, new_up, new_down)

    return local


def solution(mesh):
    feats, hids = P("row", "col"), P("col", "row")
    return jax.shard_map(
        make_local(mesh.shape["row"], mesh.shape["col"]),
        mesh=mesh,
        in_specs=(feats, feats, hids, feats, hids, feats, hids, feats),
        out_specs=(feats, hids, feats),
        check_vma=False,
    )
```
